32 devices in a mesh: dp: 4 (over y, x), ctx: 8 (over z, core).
Axes of the slice: x: 2, y: 2, z: 4, core: 2. Of those that a mesh axis runs over, the one named last changes fastest.
Arguments:
- tokens: bfloat16 [4, 4096, 2048], P('dp', 'ctx'), may hold values from -6 to 6
- w_query: bfloat16 [2048, 128], replicated, may hold values from -0.125 to 0.125
- w_key: bfloat16 [2048, 128], replicated, may hold values from -0.125 to 0.125
- w_value: bfloat16 [2048, 512], replicated, may hold values from -0.125 to 0.125
- w_out: bfloat16 [512, 2048], replicated, may hold values from -0.25 to 0.25
- grad_out: bfloat16 [4, 4096, 2048], P('dp', 'ctx'), may hold values from -6 to 6
Outputs:
- grad_tokens: bfloat16 [4, 4096, 2048], P('dp', 'ctx')
- grad_qkv: float32 [2048, 768], P(('dp', 'ctx'))
- grad_w_out: float32 [512, 2048], P(('dp', 'ctx'))
The draws below stay inside these ranges and needn't reach their ends.
All inputs are finite; a program needn't handle non-finite values.
Results may differ from the reference program's by a relative error of at most 0.013.
Values sent between devices are 32-bit elements; how exact they have to be, the bound alone decides.
A program may use at most 256 MiB of HBM per device.

```python
import math
import jax
import jax.numpy as jnp
from jax import lax

D = 2048
HEADS = 8
FEAT = 16
HDIM = 64
TOK_DEV = 512
VALW = 512
LENGTH = 4096
SEQS = 4
N_CTX = 8


def levels(rng, dims, shards, least, top_value):
    factor_of = 1.0
    for axis_at, blocks in shards:
        steps = jax.random.uniform(jax.random.fold_in(jax.random.fold_in(rng, 6), axis_at), (blocks,), jnp.float32, least / len(shards), top_value / len(shards))
        factor_of = factor_of * jnp.repeat(jnp.exp(steps), dims[axis_at] // blocks).reshape((-1,) + (1,) * (len(dims) - 1 - axis_at))
    return factor_of


def scatter_about(own_key, dims, deviation, bound, split=(), held_as=jnp.bfloat16):
    loudness = levels(own_key, dims, split, -0.22, 0.18) if split else 1.0
    values = jax.random.normal(own_key, dims, jnp.float32) * deviation * loudness
    return jnp.minimum(jnp.maximum(values, -bound), bound).astype(held_as)


def setup_inputs(seed: int = 0) -> dict:
    keys = jax.random.split(jax.random.key(seed), 7)
    tokens = scatter_about(keys[0], (SEQS, LENGTH, D), 1.0, 6.0, ((0, 4), (1, 8)))
    w_query = scatter_about(keys[1], (D, HEADS * FEAT), D ** -0.5, 0.125)
    w_key = scatter_about(keys[2], (D, HEADS * FEAT), D ** -0.5, 0.125)
    w_value = scatter_about(keys[3], (D, VALW), D ** -0.5, 0.125)
    w_out = scatter_about(keys[4], (VALW, D), VALW ** -0.5, 0.25)
    grad_out = scatter_about(keys[5], (SEQS, LENGTH, D), 1.0, 6.0, ((0, 4), (1, 8)))
    return {"tokens": tokens, "w_query": w_query, "w_key": w_key, "w_value": w_value, "w_out": w_out, "grad_out": grad_out}


SQRT_HALF = 0.7071067811865476
HIGH = lax.Precision.HIGHEST

def feature_map(vectors):
    ones = jnp.ones(vectors.shape[:-1] + (1,), vectors.dtype)
    width = vectors.shape[-1]
    square = (vectors[..., :, None] * vectors[..., None, :]).reshape(vectors.shape[:-1] + (width * width,))
    return jnp.concatenate([ones, vectors, square * SQRT_HALF], axis=-1)

def block_state(key_vec, value_vec):
    lifted = feature_map(key_vec)
    state = jnp.einsum('the,thd->hed', lifted, value_vec, precision=HIGH)
    normal = lax.optimization_barrier(jnp.sum(lifted, axis=0))
    return (state, normal)

def block_output(query_vec, key_vec, value_vec, prior_state, prior_norm):
    count = query_vec.shape[0]
    scores = jnp.einsum('thf,shf->hts', query_vec, key_vec, precision=HIGH)
    causal = (lax.broadcasted_iota(jnp.int32, (count, count), 0) >= lax.broadcasted_iota(jnp.int32, (count, count), 1)).astype(scores.dtype)
    kernel = (1.0 + scores + 0.5 * scores * scores) * causal
    lifted = feature_map(query_vec)
    numerator = jnp.einsum('hts,shd->thd', kernel, value_vec, precision=HIGH) + jnp.einsum('the,hed->thd', lifted, prior_state, precision=HIGH)
    denominator = lax.optimization_barrier(jnp.sum(kernel, axis=2)).T + jnp.einsum('the,he->th', lifted, prior_norm, precision=HIGH)
    return numerator / denominator[..., None]

def exclusive(stack, reverse):
    shaped = stack.reshape((SEQS, N_CTX) + stack.shape[1:])
    if reverse:
        shaped = jnp.flip(shaped, axis=1)
    running = jnp.cumsum(shaped, axis=1)
    shifted = jnp.concatenate([jnp.zeros_like(shaped[:, :1]), running[:, :-1]], axis=1)
    if reverse:
        shifted = jnp.flip(shifted, axis=1)
    return shifted.reshape(stack.shape)

def transposed_dot(left, weight):
    return lax.dot_general(left, weight, (((1,), (1,)), ((), ())), preferred_element_type=jnp.float32)

def backward_block(packed):
    query_vec, key_vec, value_vec, prior_state, prior_norm, cotangent = packed
    outputs, backward = jax.vjp(block_output, query_vec, key_vec, value_vec, prior_state, prior_norm)
    grads = backward(cotangent)
    return (outputs.astype(jnp.bfloat16),) + tuple(grads)

def state_block(packed):
    key_vec, value_vec, later_state, later_norm = packed
    unused, state_back = jax.vjp(block_state, key_vec, value_vec)
    return state_back((later_state, later_norm))

def reference(tokens, w_query, w_key, w_value, w_out, grad_out):
    token_rows = tokens.reshape(-1, D)
    grad_rows = grad_out.reshape(-1, D)
    blocks = SEQS * N_CTX
    queries = (jnp.dot(token_rows, w_query, preferred_element_type=jnp.float32) * 0.5).astype(jnp.bfloat16)
    keys_all = (jnp.dot(token_rows, w_key, preferred_element_type=jnp.float32) * 0.5).astype(jnp.bfloat16)
    values_all = jnp.dot(token_rows, w_value, preferred_element_type=jnp.float32).astype(jnp.bfloat16)
    query_vec = queries.astype(jnp.float32).reshape(blocks, TOK_DEV, HEADS, FEAT)
    key_vec = keys_all.astype(jnp.float32).reshape(blocks, TOK_DEV, HEADS, FEAT)
    value_vec = values_all.astype(jnp.float32).reshape(blocks, TOK_DEV, HEADS, HDIM)
    states, norms = lax.map(lambda packed: block_state(packed[0], packed[1]), (key_vec, value_vec))
    prior_state = exclusive(states, False)
    prior_norm = exclusive(norms, False)
    grad_attn = transposed_dot(grad_rows, w_out).reshape(blocks, TOK_DEV, HEADS, HDIM)
    attended, grad_query, grad_key_own, grad_value_own, grad_state, grad_norm = lax.map(backward_block, (query_vec, key_vec, value_vec, prior_state, prior_norm, grad_attn))
    later_state = exclusive(grad_state, True)
    later_norm = exclusive(grad_norm, True)
    grad_key_far, grad_value_far = lax.map(state_block, (key_vec, value_vec, later_state, later_norm))
    rows = SEQS * LENGTH
    proj_query = (grad_query * 0.5).reshape(rows, -1).astype(jnp.bfloat16)
    proj_key = ((grad_key_own + grad_key_far) * 0.5).reshape(rows, -1).astype(jnp.bfloat16)
    proj_value = (grad_value_own + grad_value_far).reshape(rows, -1).astype(jnp.bfloat16)
    grad_tokens = (transposed_dot(proj_query, w_query) + transposed_dot(proj_key, w_key) + transposed_dot(proj_value, w_value)).astype(jnp.bfloat16)
    scale = 1.0 / math.sqrt(SEQS * LENGTH)
    stacked = jnp.concatenate([proj_query, proj_key, proj_value], axis=1)
    grad_qkv = lax.dot_general(token_rows, stacked, (((0,), (0,)), ((), ())), preferred_element_type=jnp.float32) * scale
    attended_rows = attended.reshape(rows, VALW)
    grad_w_out = lax.dot_general(attended_rows, grad_rows, (((0,), (0,)), ((), ())), preferred_element_type=jnp.float32) * scale
    return (grad_tokens.reshape(SEQS, LENGTH, D), grad_qkv, grad_w_out)
```

```python
import functools
import math

import jax
import jax.numpy as jnp
from jax import lax
from jax.experimental import pallas as pl
from jax.experimental.pallas import tpu as pltpu
from jax.sharding import PartitionSpec as P

HEADS = 8
FEAT = 16
HDIM = 64
PAIRS = HEADS // 2
LIFT = 160
SQRT_HALF = 0.7071067811865476
F32 = jnp.float32
BF16 = jnp.bfloat16
MESH = pl.DeviceIdType.MESH
VMEM_LIMIT = 56 * 2**20


def dot_nn(a, b):
    return lax.dot_general(a, b, (((1,), (0,)), ((), ())), preferred_element_type=F32)


def dot_nt(a, b):
    return lax.dot_general(a, b, (((1,), (1,)), ((), ())), preferred_element_type=F32)


def dot_tn(a, b):
    return lax.dot_general(a, b, (((0,), (0,)), ((), ())), preferred_element_type=F32)


def shifted(u, d):
    return u if d == 0 else jnp.concatenate([u[d:], u[:d]], axis=0)


def lift(u):
    count = u.shape[1]
    rows = [u * u * SQRT_HALF]
    for d in range(1, FEAT // 2):
        rows.append(u * shifted(u, d))
    rows.append(u[: FEAT // 2] * u[FEAT // 2 :])
    first = lax.broadcasted_iota(jnp.int32, (8, count), 0) == 0
    rows.append(jnp.where(first, 1.0, 0.0).astype(F32))
    rows.append(u)
    return jnp.concatenate(rows, axis=0)


def unlift(grad, u):
    out = grad[LIFT - FEAT :] + (2.0 * SQRT_HALF) * grad[:FEAT] * u
    for d in range(1, FEAT // 2):
        part = grad[d * FEAT : (d + 1) * FEAT]
        out = out + part * shifted(u, d) + shifted(part * u, FEAT - d)
    half = FEAT // 2
    part = grad[half * FEAT : half * FEAT + half]
    return out + jnp.concatenate([part * u[half:], part * u[:half]], axis=0)


def split(x):
    high = x.astype(BF16)
    return high, (x - high.astype(F32)).astype(BF16)


def stack_rows(rows, count):
    pad = jnp.zeros((16 - len(rows), count), F32)
    return jnp.concatenate([r.astype(F32) for r in rows] + [pad], axis=0).astype(BF16)


def state_kernel(k_ref, v_ref, s_ref, n_ref):
    sums, norms = [], []
    count = k_ref.shape[1]
    for h in range(2):
        lifted = lift(k_ref[h * FEAT : (h + 1) * FEAT, :].astype(F32)).astype(BF16)
        sums.append(dot_nt(lifted, v_ref[h * HDIM : (h + 1) * HDIM, :]))
        norms.append(dot_nt(jnp.ones((8, count), BF16), lifted)[:1])
    s_ref[0] = jnp.concatenate(sums, axis=1)
    n_ref[0] = jnp.concatenate(norms + [jnp.zeros((6, LIFT), F32)], axis=0)


def attend_kernel(q_ref, k_ref, v_ref, g_ref, s_ref, n_ref, a_ref, gq_ref, gk_ref, gv_ref, ds_ref, dn_ref):
    count = q_ref.shape[1]
    later = lax.broadcasted_iota(jnp.int32, (count, count), 1) >= lax.broadcasted_iota(
        jnp.int32, (count, count), 0
    )
    sums, norms = [], []
    for h in range(2):
        small = slice(h * FEAT, (h + 1) * FEAT)
        wide = slice(h * HDIM, (h + 1) * HDIM)
        q, k, v = q_ref[small, :], k_ref[small, :], v_ref[wide, :]
        state = s_ref[0, :, wide].astype(BF16)
        n_high, n_low = split(n_ref[0, h : h + 1, :])
        score = dot_tn(k, q)
        kernel = jnp.where(later, 1.0 + score + 0.5 * score * score, 0.0)
        kernel_b = kernel.astype(BF16)
        u = q.astype(F32)
        lifted = lift(u).astype(BF16)
        top = dot_nn(v, kernel_b) + dot_tn(state, lifted)
        prior = dot_nn(stack_rows([n_high, n_low], LIFT), lifted)
        below = jnp.sum(kernel, axis=0, keepdims=True) + prior[0:1] + prior[1:2]
        inverse = 1.0 / below
        attention = top * inverse
        a_ref[wide, :] = attention.astype(BF16)
        g = g_ref[wide, :] * inverse
        below_grad = -jnp.sum(g * attention, axis=0, keepdims=True)
        g_b = g.astype(BF16)
        b_high, b_low = split(below_grad)
        kernel_grad = dot_tn(v, g_b) + below_grad
        score_grad = jnp.where(later, kernel_grad * (1.0 + score), 0.0).astype(BF16)
        lift_grad = dot_nn(state, g_b) + dot_tn(
            stack_rows([n_high, n_low, n_high], LIFT), stack_rows([b_high, b_high, b_low], count)
        )
        gq_ref[small, :] = ((dot_nn(k, score_grad) + unlift(lift_grad, u)) * 0.5).astype(BF16)
        gk_ref[small, :] = dot_nt(q, score_grad)
        gv_ref[wide, :] = dot_nt(g_b, kernel_b)
        sums.append(dot_nt(lifted, g_b))
        pair = dot_nt(stack_rows([b_high, b_low], count), lifted)
        norms.append(pair[0:1] + pair[1:2])
    ds_ref[0] = jnp.concatenate(sums, axis=1)
    dn_ref[0] = jnp.concatenate(norms + [jnp.zeros((6, LIFT), F32)], axis=0)


def far_kernel(k_ref, v_ref, gk_ref, gv_ref, s_ref, n_ref, pk_ref, pv_ref):
    count = k_ref.shape[1]
    for h in range(2):
        small = slice(h * FEAT, (h + 1) * FEAT)
        wide = slice(h * HDIM, (h + 1) * HDIM)
        u = k_ref[small, :].astype(F32)
        lifted = lift(u).astype(BF16)
        state = s_ref[0, :, wide].astype(BF16)
        n_high, n_low = split(n_ref[0, h : h + 1, :])
        ones = jnp.ones((1, count), F32)
        lift_grad = dot_nn(state, v_ref[wide, :]) + dot_tn(
            stack_rows([n_high, n_low], LIFT), stack_rows([ones, ones], count)
        )
        pk_ref[small, :] = ((gk_ref[small, :] + unlift(lift_grad, u)) * 0.5).astype(BF16)
        pv_ref[wide, :] = (gv_ref[wide, :] + dot_tn(state, lifted)).astype(BF16)


def rows_spec(rows, count):
    return pl.BlockSpec((rows, count), lambda p: (p, 0))


def pair_spec(rows, columns):
    return pl.BlockSpec((1, rows, columns), lambda p: (p, 0, 0))


def flipped(index, bit):
    return index + bit - 2 * bit * lax.rem(lax.div(index, bit), 2)


def bits_of(size):
    return [1 << b for b in range(size.bit_length() - 1)]


def enter(partners):
    barrier = pltpu.get_barrier_semaphore()
    for partner in partners:
        pl.semaphore_signal(barrier, inc=1, device_id=partner, device_id_type=MESH)
    pl.semaphore_wait(barrier, len(partners))


def scan_kernel(size, backward, s_ref, n_ref, so_ref, no_ref, s_sum, n_sum, s_got, n_got, send, recv):
    dp, me = lax.axis_index("dp"), lax.axis_index("ctx")
    bits = bits_of(size)
    partners = [(dp, flipped(me, bit)) for bit in bits]
    enter(partners)
    for at, (bit, partner) in enumerate(zip(bits, partners)):
        last = at == len(bits) - 1
        mine = ((s_ref if at == 0 else s_sum.at[at % 2]), (n_ref if at == 0 else n_sum.at[at % 2]))
        copies = [
            pltpu.make_async_remote_copy(
                src_ref=source,
                dst_ref=target.at[at],
                send_sem=send.at[at, i],
                recv_sem=recv.at[at, i],
                device_id=partner,
                device_id_type=MESH,
            )
            for i, (source, target) in enumerate(zip(mine, (s_got, n_got)))
        ]
        for copy in copies:
            copy.start()
        upper = lax.rem(lax.div(me, bit), 2)
        takes = (1 - upper if backward else upper).astype(F32)
        for copy in copies:
            copy.wait()
        for got, held, total, out in (
            (s_got, mine[0], s_sum, so_ref),
            (n_got, mine[1], n_sum, no_ref),
        ):
            arrived = got[at]
            out[...] = arrived * takes if at == 0 else out[...] + arrived * takes
            if not last:
                total[(at + 1) % 2] = held[...] + arrived


def carried(state, norm, size, backward, call):
    steps = len(bits_of(size))
    vmem = pl.BlockSpec(memory_space=pltpu.VMEM)
    return pl.pallas_call(
        functools.partial(scan_kernel, size, backward),
        out_shape=(
            jax.ShapeDtypeStruct(state.shape, F32),
            jax.ShapeDtypeStruct(norm.shape, F32),
        ),
        in_specs=[vmem, vmem],
        out_specs=(vmem, vmem),
        scratch_shapes=[
            pltpu.VMEM((2,) + state.shape, F32),
            pltpu.VMEM((2,) + norm.shape, F32),
            pltpu.VMEM((steps,) + state.shape, F32),
            pltpu.VMEM((steps,) + norm.shape, F32),
            pltpu.SemaphoreType.DMA((steps, 2)),
            pltpu.SemaphoreType.DMA((steps, 2)),
        ],
        compiler_params=pltpu.CompilerParams(
            collective_id=call, has_side_effects=True, vmem_limit_bytes=VMEM_LIMIT
        ),
    )(state, norm)


def scatter_kernel(dp_size, ctx_size, arrays, *refs):
    dp, me = lax.axis_index("dp"), lax.axis_index("ctx")
    ins, outs = refs[:arrays], refs[arrays : 2 * arrays]
    held = refs[2 * arrays : 4 * arrays]
    got = refs[4 * arrays : 6 * arrays]
    send, recv, load = refs[6 * arrays :]
    dp_bits = [("dp", b) for b in bits_of(dp_size)]
    ctx_bits = [("ctx", b) for b in bits_of(ctx_size)]
    orders = [ctx_bits[:1] + dp_bits + ctx_bits[1:], ctx_bits[:1] + dp_bits[::-1] + ctx_bits[1:]]
    steps = len(orders[0])

    def partner_of(axis, bit):
        return (flipped(dp, bit), me) if axis == "dp" else (dp, flipped(me, bit))

    enter([partner_of(*bit) for bit in orders[0]])
    slots = 1 << steps

    def block_of(order, slot):
        d, c = dp, me
        for at, (axis, bit) in enumerate(order):
            if slot >> (steps - 1 - at) & 1:
                d, c = (flipped(d, bit), c) if axis == "dp" else (d, flipped(c, bit))
        return d * ctx_size + c

    half = slots // 2
    for part, order in enumerate(orders):
        for a in range(arrays):
            buf = 2 * a + part
            rows, columns = held[buf].shape[1:]
            across = pl.ds(part * columns, columns)
            for slot in range(half):
                block = block_of(order, half + slot)
                pltpu.make_async_remote_copy(
                    src_ref=ins[a].at[pl.ds(block * rows, rows), across],
                    dst_ref=got[buf].at[slot],
                    send_sem=send.at[0, buf],
                    recv_sem=recv.at[0, buf],
                    device_id=partner_of(*order[0]),
                    device_id_type=MESH,
                ).start()
            for slot in range(half):
                block = block_of(order, slot)
                pltpu.make_async_copy(
                    ins[a].at[pl.ds(block * rows, rows), across], held[buf].at[slot], load.at[buf]
                ).start()

    def step_copy(at, buf, order):
        keep = slots >> (at + 1)
        if at == 0:
            source, target = held[buf], got[buf].at[pl.ds(0, half)]
        else:
            source = held[buf].at[pl.ds(keep, keep)]
            target = got[buf].at[pl.ds(slots - 2 * keep, keep)]
        return pltpu.make_async_remote_copy(
            src_ref=source,
            dst_ref=target,
            send_sem=send.at[at, buf],
            recv_sem=recv.at[at, buf],
            device_id=partner_of(*order[at]),
            device_id_type=MESH,
        )

    bufs = [(2 * a + part, orders[part]) for a in range(arrays) for part in range(2)]
    for at in range(steps):
        keep = slots >> (at + 1)
        for buf, order in bufs:
            if at == 0:
                pltpu.make_async_copy(held[buf], held[buf], load.at[buf]).wait()
            step_copy(at, buf, order).wait()
            base = slots - 2 * keep
            if at == steps - 1:
                a, part = buf // 2, buf % 2
                columns = held[buf].shape[2]
                outs[a][:, part * columns : (part + 1) * columns] = held[buf][0] + got[buf][base]
                continue
            near = keep // 2

            def add(slot, carry, buf=buf, base=base):
                held[buf][slot] = held[buf][slot] + got[buf][base + slot]
                return carry

            lax.fori_loop(near, keep, add, 0)
            step_copy(at + 1, buf, order).start()
            lax.fori_loop(0, near, add, 0)


def scattered(parts, dp_size, ctx_size, call):
    devices = dp_size * ctx_size
    half = devices // 2
    steps = len(bits_of(devices))
    blocks = [(p.shape[0] // devices, p.shape[1]) for p in parts]
    bufs = [(b[0], b[1] // 2) for b in blocks for _ in range(2)]
    hbm = pl.BlockSpec(memory_space=pl.ANY)
    vmem = pl.BlockSpec(memory_space=pltpu.VMEM)
    return pl.pallas_call(
        functools.partial(scatter_kernel, dp_size, ctx_size, len(parts)),
        out_shape=tuple(jax.ShapeDtypeStruct(b, F32) for b in blocks),
        in_specs=[hbm] * len(parts),
        out_specs=(vmem,) * len(parts),
        scratch_shapes=[pltpu.VMEM((half,) + b, F32) for b in bufs]
        + [pltpu.VMEM((devices - 1,) + b, F32) for b in bufs]
        + [
            pltpu.SemaphoreType.DMA((steps, len(bufs))),
            pltpu.SemaphoreType.DMA((steps, len(bufs))),
            pltpu.SemaphoreType.DMA((len(bufs),)),
        ],
        compiler_params=pltpu.CompilerParams(
            collective_id=call, has_side_effects=True, vmem_limit_bytes=VMEM_LIMIT
        ),
    )(*parts)


def shards(tokens, w_query, w_key, w_value, w_out, grad_out):
    token_rows = tokens.reshape(-1, tokens.shape[-1])
    grad_rows = grad_out.reshape(-1, grad_out.shape[-1])
    count = token_rows.shape[0]
    dp_size, ctx_size = lax.axis_size("dp"), lax.axis_size("ctx")
    narrow, broad = HEADS * FEAT, HEADS * HDIM
    weights = jnp.concatenate([w_query, w_key, w_value], axis=1)
    factor = jnp.where(jnp.arange(weights.shape[1]) < 2 * narrow, 0.5, 1.0)[:, None]
    projected = (
        lax.dot_general(weights, token_rows, (((0,), (1,)), ((), ())), preferred_element_type=F32)
        * factor
    ).astype(BF16)
    q, k, v = projected[:narrow], projected[narrow : 2 * narrow], projected[2 * narrow :]
    g = dot_nt(w_out, grad_rows)
    small, wide = rows_spec(2 * FEAT, count), rows_spec(2 * HDIM, count)
    state_block, norm_block = pair_spec(LIFT, 2 * HDIM), pair_spec(8, LIFT)
    state_shape = jax.ShapeDtypeStruct((PAIRS, LIFT, 2 * HDIM), F32)
    norm_shape = jax.ShapeDtypeStruct((PAIRS, 8, LIFT), F32)
    params = pltpu.CompilerParams(vmem_limit_bytes=VMEM_LIMIT)
    state, norm = pl.pallas_call(
        state_kernel,
        grid=(PAIRS,),
        out_shape=(state_shape, norm_shape),
        in_specs=[small, wide],
        out_specs=(state_block, norm_block),
        compiler_params=params,
    )(k, v)
    state, norm = carried(state, norm, ctx_size, False, 0)
    attended, proj_query, grad_key, grad_value, state, norm = pl.pallas_call(
        attend_kernel,
        grid=(PAIRS,),
        out_shape=(
            jax.ShapeDtypeStruct((broad, count), BF16),
            jax.ShapeDtypeStruct((narrow, count), BF16),
            jax.ShapeDtypeStruct((narrow, count), F32),
            jax.ShapeDtypeStruct((broad, count), F32),
            state_shape,
            norm_shape,
        ),
        in_specs=[small, small, wide, wide, state_block, norm_block],
        out_specs=(wide, small, small, wide, state_block, norm_block),
        compiler_params=params,
    )(q, k, v, g, state, norm)
    state, norm = carried(state, norm, ctx_size, True, 1)
    proj_key, proj_value = pl.pallas_call(
        far_kernel,
        grid=(PAIRS,),
        out_shape=(
            jax.ShapeDtypeStruct((narrow, count), BF16),
            jax.ShapeDtypeStruct((broad, count), BF16),
        ),
        in_specs=[small, wide, small, wide, state_block, norm_block],
        out_specs=(small, wide),
        compiler_params=params,
    )(k, v, grad_key, grad_value, state, norm)
    scale = 1.0 / math.sqrt(dp_size * ctx_size * count)
    stacked = jnp.concatenate([proj_query, proj_key, proj_value], axis=0)
    grad_tokens = lax.dot_general(
        stacked, weights, (((0,), (1,)), ((), ())), preferred_element_type=F32
    ).astype(BF16)
    part_qkv = (
        lax.dot_general(token_rows, stacked, (((0,), (1,)), ((), ())), preferred_element_type=F32)
        * scale
    )
    part_out = dot_nn(attended, grad_rows) * scale
    grad_qkv, grad_w_out = scattered([part_qkv, part_out], dp_size, ctx_size, 2)
    return (grad_tokens.reshape(tokens.shape), grad_qkv, grad_w_out)


def solution(mesh):
    placed = (P("dp", "ctx", None), P(), P(), P(), P(), P("dp", "ctx", None))
    return jax.shard_map(
        shards,
        mesh=mesh,
        in_specs=placed,
        out_specs=(P("dp", "ctx", None), P(("dp", "ctx"), None), P(("dp", "ctx"), None)),
        check_vma=False,
    )
```
